32 devices in a mesh: rep: 4 (over z), sp: 8 (over y, x, core).
Axes of the slice: x: 2, y: 2, z: 4, core: 2. Of those that a mesh axis runs over, the one named last changes fastest.
Arguments:
- inputs: bfloat16 [4, 8, 16, 4096], P('rep', 'sp'), may hold values from -6 to 6
- preact: bfloat16 [4, 8, 16, 4096], P('rep', 'sp'), may hold values from -6 to 6
- grad_out: bfloat16 [4, 8, 16, 4096], P('rep', 'sp'), may hold values from -20 to 20
- weight: bfloat16 [3, 3, 3, 64, 64], replicated, may hold values from -0.15625 to 0.15625
Outputs:
- input_grad: bfloat16 [4, 8, 16, 4096], P('rep', 'sp')
- weight_grad: float32 [3, 3, 3, 64, 64], replicated
- bias_grad: float32 [64], replicated
The draws below stay inside these ranges and needn't reach their ends.
All inputs are finite; a program needn't handle non-finite values.
Results may differ from the reference program's by a relative error of at most 0.001.
Values may be sent and summed in bfloat16 or wider, within the bound.
A program may use at most 64 MiB of HBM per device.

```python
import jax
import jax.numpy as jnp
from jax import lax

CH = 64
WIDTH = 64
HEIGHT = 16
BATCH = 4
DEPTH = 8


def draw_grad_out(key, part):
    shape = (BATCH, DEPTH, HEIGHT, WIDTH * CH)
    first = jax.random.fold_in(key, 0)
    base = jax.random.normal(first, shape, jnp.float32)
    position = jnp.arange(DEPTH, dtype=jnp.float32) / max(DEPTH - 1, 1)
    factor = jnp.exp(position * jnp.log(3.0))
    return jnp.clip(base * factor[None, :, None, None], -20.0, 20.0).astype(jnp.bfloat16)


def levels(stream_key, dims, cuts, smallest, high):
    loudness, own = 1.0, jax.random.fold_in(stream_key, 6)
    for axis_at, blocks in cuts:
        heights = jnp.exp(jax.random.uniform(jax.random.fold_in(own, axis_at), (blocks,), jnp.float32, smallest / len(cuts), high / len(cuts)))
        loudness = loudness * jnp.repeat(heights, dims[axis_at] // blocks).reshape([-1 if axis == axis_at else 1 for axis in range(len(dims))])
    return loudness


def centred(own_key, dims, spread, most, shards=(), kind=jnp.bfloat16):
    level = levels(own_key, dims, shards, -0.22, 0.18) if shards else 1.0
    array = jax.random.normal(own_key, dims, jnp.float32) * spread * level
    return jnp.minimum(jnp.maximum(array, -most), most).astype(kind)


def setup_inputs(seed: int = 0) -> dict:
    seeds = jax.random.split(jax.random.key(seed), 5)
    inputs = centred(seeds[0], (BATCH, DEPTH, HEIGHT, WIDTH * CH), 1.0, 6.0, ((0, 4), (1, 8)))
    preact = centred(seeds[1], (BATCH, DEPTH, HEIGHT, WIDTH * CH), 1.0, 6.0, ((0, 4), (1, 8)))
    grad_out = draw_grad_out(jax.random.fold_in(seeds[4], 71), 0)
    weight = centred(seeds[3], (3, 3, 3, CH, CH), (27 * CH) ** -0.5, 0.15625)
    return {"inputs": inputs, "preact": preact, "grad_out": grad_out, "weight": weight}


def unfold(volume, channels):
    samples, planes, height, packed = volume.shape
    cells = packed // channels
    shaped = volume.reshape(samples, planes, height, cells, channels)
    padded = jnp.pad(shaped, ((0, 0), (0, 0), (1, 1), (1, 1), (0, 0)))
    pieces = []
    for tap_h in range(3):
        for tap_w in range(3):
            pieces.append(padded[:, :, tap_h:tap_h + height, tap_w:tap_w + cells, :])
    stacked = jnp.concatenate(pieces, axis=4)
    return stacked.reshape(-1, 9 * channels)


def reference(inputs, preact, grad_out, weight):
    channels = weight.shape[3]
    flipped = jnp.transpose(weight[::-1, ::-1, ::-1], (0, 1, 2, 4, 3))

    def one_sample(operands):
        x_one, z_one, dy_one = operands
        x_one = x_one[None]
        grad_masked = jnp.where(z_one[None] > 0, dy_one[None], jnp.zeros_like(dy_one[None]))
        planes = x_one.shape[1]
        grad_padded = jnp.pad(grad_masked, ((0, 0), (1, 1), (0, 0), (0, 0)))
        input_padded = jnp.pad(x_one, ((0, 0), (1, 1), (0, 0), (0, 0)))
        grad_flat = grad_masked.reshape(-1, channels)
        totals = jnp.zeros((grad_flat.shape[0], channels), jnp.float32)
        kernel_rows = []
        for depth_tap in range(3):
            grad_cols = unfold(grad_padded[:, depth_tap:depth_tap + planes], channels)
            totals = totals + jnp.dot(grad_cols, flipped[depth_tap].reshape(9 * channels, channels), preferred_element_type=jnp.float32)
            input_cols = unfold(input_padded[:, depth_tap:depth_tap + planes], channels)
            part = lax.dot_general(input_cols, grad_flat, (((0,), (0,)), ((), ())), preferred_element_type=jnp.float32)
            kernel_rows.append(part.reshape(3, 3, channels, channels))
        dx_one = totals.reshape(grad_masked.shape[1:]).astype(jnp.bfloat16)
        dw_one = jnp.stack(kernel_rows, axis=0)
        db_one = jnp.sum(grad_flat.astype(jnp.float32), axis=0)
        return dx_one, dw_one, db_one

    input_grad, kernel_each, bias_each = lax.map(one_sample, (inputs, preact, grad_out))
    scale = 1.0 / (BATCH * DEPTH * HEIGHT * WIDTH) ** 0.5
    weight_grad = jnp.sum(kernel_each, axis=0) * scale
    bias_grad = jnp.sum(bias_each, axis=0) * scale
    return input_grad, weight_grad, bias_grad
```

```python
import functools

import jax
import jax.numpy as jnp
from jax import lax
from jax.experimental import pallas as pl
from jax.experimental.pallas import tpu as pltpu
from jax.sharding import PartitionSpec as P

MESH = pl.DeviceIdType.MESH
F32 = jnp.float32
BF16 = jnp.bfloat16


def round_up(value, step):
    return -(-value // step) * step


def to_rows(plane, lanes):
    count = plane.shape[1] // lanes
    return jnp.concatenate([plane[:, j * lanes : (j + 1) * lanes] for j in range(count)], axis=0)


def shift_rows(rows, offset, height):
    place = lax.broadcasted_iota(jnp.int32, rows.shape, 0) % height
    moved = pltpu.roll(rows, (-offset) % rows.shape[0], 0)
    inside = (place + offset >= 0) & (place + offset < height)
    return jnp.where(inside, moved, jnp.zeros_like(moved))


def kernel(
    n_rep, n_sp, scale,
    x_ref, z_ref, dy_ref, w_ref,
    dx_ref, wg_ref, bg_ref,
    gbuf, halo, xt, wn, gc, acc, pair_in, mid, xy_in, z_in, z_own, z_all, full,
    halo_send, halo_recv, pair_send, pair_recv, xy_send, xy_recv, z_send, z_recv,
    zg_send, zg_recv, xg_send, xg_recv, pg_send, pg_recv,
):
    height = x_ref.shape[2]
    ch = w_ref.shape[3]
    lanes = 2 * ch
    rows = height * x_ref.shape[3] // lanes
    n_chip = n_sp // 2
    part = xy_in.shape[1]
    half = n_chip * part
    zpart = z_in.shape[1]

    rep, sp = lax.axis_index("rep"), lax.axis_index("sp")
    core, chip = sp % 2, sp // 2
    pair = chip * 2 + 1 - core
    far = sp + 2 * core - 1
    has_far = (far >= 0) & (far < n_sp)

    def chip_at(step):
        return lax.rem(chip + step, n_chip)

    def rep_at(step):
        return lax.rem(rep + step, n_rep)

    barrier = pltpu.get_barrier_semaphore()

    def greet(**where):
        pl.semaphore_signal(barrier, inc=1, device_id=where, device_id_type=MESH)

    greet(sp=pair)
    for t in range(1, n_chip):
        greet(sp=chip_at(t) * 2 + core)
    for t in range(1, n_rep):
        greet(rep=rep_at(t))

    @pl.when(has_far)
    def _():
        greet(sp=far)

    keep = z_ref[0, 0].astype(F32) > 0
    g_plane = jnp.where(keep, dy_ref[0, 0].astype(F32), 0.0)
    gbuf[...] = g_plane.astype(BF16)

    pl.semaphore_wait(barrier, n_chip + n_rep - 1 + jnp.where(has_far, 1, 0))

    def copy(src, dst, send, recv, **where):
        return pltpu.make_async_remote_copy(
            src_ref=src, dst_ref=dst, send_sem=send, recv_sem=recv,
            device_id=where, device_id_type=MESH,
        )

    near_copy = copy(gbuf, halo.at[core], halo_send.at[0], halo_recv.at[0], sp=pair)
    far_copy = copy(gbuf, halo.at[1 - core], halo_send.at[1], halo_recv.at[1], sp=far)

    @pl.when(has_far)
    def _():
        far_copy.start()

    near_copy.start()

    @pl.when(jnp.logical_not(has_far))
    def _():
        halo[core] = jnp.zeros_like(gbuf)

    x_rows = to_rows(x_ref[0, 0].astype(F32), lanes)
    for k, oh in enumerate((-1, 0, 1)):
        xt[k * lanes : (k + 1) * lanes, :] = shift_rows(x_rows, oh, height).astype(BF16).T

    zero_tap = jnp.zeros((ch, ch), BF16)
    for od in range(3):
        for oh in range(3):
            w_m, w_0, w_p = w_ref[od, oh, 0], w_ref[od, oh, 1], w_ref[od, oh, 2]
            r, c = oh * lanes, od * 2 * lanes
            grid = ((w_0, w_m, w_p, zero_tap), (w_p, w_0, zero_tap, w_m))
            for a in range(2):
                for b in range(4):
                    wn[r + a * ch : r + (a + 1) * ch, c + b * ch : c + (b + 1) * ch] = grid[a][b]

    left = lax.broadcasted_iota(jnp.int32, (rows, lanes), 1) < ch
    left_tile = lax.broadcasted_iota(jnp.int32, (ch, lanes), 1) < ch

    def spread(g_rows, od):
        turned = pltpu.roll(g_rows, ch, 1)
        gap = jnp.zeros((height, lanes), F32)
        before = jnp.concatenate([gap, turned[:-height]], axis=0)
        after = jnp.concatenate([turned[height:], gap], axis=0)
        c = od * 2 * lanes
        gc[:, c : c + lanes] = g_rows.astype(BF16)
        gc[:, c + lanes : c + 2 * lanes] = jnp.where(left, before, after).astype(BF16)

    middles = [None] * 9

    def taps(od):
        c = od * 2 * lanes
        prod = jnp.dot(xt[...], gc[:, c : c + 2 * lanes], preferred_element_type=F32)
        for oh in range(3):
            r = oh * lanes
            own0, own1 = prod[r : r + ch, :lanes], prod[r + ch : r + 2 * ch, :lanes]
            mix0, mix1 = prod[r : r + ch, lanes:], prod[r + ch : r + 2 * ch, lanes:]
            u = od * 3 + oh
            acc[u * ch : (u + 1) * ch, :] = jnp.where(left_tile, own1 + mix0, own0 + mix1)
            same = jnp.where(left_tile, own0, own1)
            middles[u] = same + pltpu.roll(same, ch, 1)

    g_rows = to_rows(g_plane, lanes)
    spread(g_rows, 1)
    taps(1)
    bias = jnp.sum(g_rows, axis=0, keepdims=True)
    bias = bias + pltpu.roll(bias, ch, 1)

    near_copy.wait_recv()

    @pl.when(has_far)
    def _():
        far_copy.wait_recv()

    spread(to_rows(halo[1].astype(F32), lanes), 0)
    spread(to_rows(halo[0].astype(F32), lanes), 2)
    taps(0)
    taps(2)
    others = middles + [jnp.broadcast_to(bias, (ch, lanes))]
    for m in range(5):
        u = 9 + m
        acc[u * ch : (u + 1) * ch, :] = jnp.where(left_tile, others[2 * m], others[2 * m + 1])
    if acc.shape[0] > 14 * ch:
        acc[14 * ch :, :] = jnp.zeros((acc.shape[0] - 14 * ch, lanes), F32)

    theirs = acc.at[pl.ds(pl.multiple_of((1 - core) * half, 8), half)]
    pair_copy = copy(theirs, pair_in, pair_send, pair_recv, sp=pair)
    pair_copy.start()

    step = 8 * height
    for s in range(0, rows, step):
        y = lax.dot_general(
            gc[s : s + step, :], wn[...], (((1,), (1,)), ((), ())), preferred_element_type=F32
        )
        total = y[:, lanes : 2 * lanes]
        total = total + shift_rows(y[:, :lanes], 1, height)
        total = total + shift_rows(y[:, 2 * lanes :], -1, height)
        total = total.astype(BF16)
        for j in range(step // height):
            c = (s // height + j) * lanes
            dx_ref[0, 0, :, c : c + lanes] = total[j * height : (j + 1) * height]

    pair_copy.wait_recv()
    mid[...] = acc[pl.ds(pl.multiple_of(core * half, 8), half), :] + pair_in[...]

    xy_copies = []
    for t in range(1, n_chip):
        to = chip_at(t)
        block = mid.at[pl.ds(pl.multiple_of(to * part, 8), part)]
        c = copy(block, xy_in.at[t - 1], xy_send.at[t - 1], xy_recv.at[t - 1], sp=to * 2 + core)
        c.start()
        xy_copies.append(c)
    own = mid[pl.ds(pl.multiple_of(chip * part, 8), part), :]
    for t in range(1, n_chip):
        xy_copies[t - 1].wait_recv()
        own = own + xy_in[t - 1]
    z_own[...] = own

    def z_start(k):
        return pl.multiple_of(jnp.minimum(k * zpart, part - zpart), 8)

    z_copies = []
    for t in range(1, n_rep):
        to = rep_at(t)
        block = z_own.at[pl.ds(z_start(to), zpart)]
        c = copy(block, z_in.at[rep], z_send.at[t - 1], z_recv.at[t - 1], rep=to)
        c.start()
        z_copies.append(c)
    z_in[rep] = z_own[pl.ds(z_start(rep), zpart), :]
    for c in z_copies:
        c.wait_recv()
    z_all[rep] = functools.reduce(lambda p, q: p + q, [z_in[k] for k in range(n_rep)]) * scale

    zg_copies = []
    for t in range(1, n_rep):
        c = copy(z_all.at[rep], z_all.at[rep], zg_send.at[t - 1], zg_recv.at[t - 1], rep=rep_at(t))
        c.start()
        zg_copies.append(c)
    for c in zg_copies:
        c.wait_recv()
    for k in range(n_rep):
        at = min(k * zpart, part - zpart)
        full[core, chip, at : at + zpart, :] = z_all[k]

    mine = full.at[core, chip]
    xg_copies = []
    for t in range(1, n_chip):
        c = copy(mine, mine, xg_send.at[t - 1], xg_recv.at[t - 1], sp=chip_at(t) * 2 + core)
        c.start()
        xg_copies.append(c)
    pg_copies = [copy(mine, mine, pg_send.at[0], pg_recv.at[0], sp=pair)]
    pg_copies[0].start()
    for t in range(1, n_chip):
        xg_copies[t - 1].wait_recv()
        came = full.at[core, lax.rem(chip + n_chip - t, n_chip)]
        c = copy(came, came, pg_send.at[t], pg_recv.at[t], sp=pair)
        c.start()
        pg_copies.append(c)
    for c in pg_copies:
        c.wait_recv()

    flat = full.reshape(2 * half, lanes)
    for od in range(3):
        for oh in range(3):
            u = od * 3 + oh
            tile = flat[u * ch : (u + 1) * ch, :]
            wg_ref[od, oh, 2] = tile[:, :ch]
            wg_ref[od, oh, 0] = tile[:, ch:]
            v = 9 + u // 2
            tile = flat[v * ch : (v + 1) * ch, :]
            wg_ref[od, oh, 1] = tile[:, :ch] if u % 2 == 0 else tile[:, ch:]
    bg_ref[...] = flat[13 * ch : 13 * ch + 1, :][:, ch:]

    near_copy.wait_send()

    @pl.when(has_far)
    def _():
        far_copy.wait_send()

    for c in [pair_copy] + xy_copies + z_copies + zg_copies + xg_copies + pg_copies:
        c.wait_send()


def on_device(n_rep, n_sp, inputs, preact, grad_out, weight):
    ch = weight.shape[3]
    height, packed = inputs.shape[2:]
    lanes = 2 * ch
    rows = height * packed // lanes
    n_chip = n_sp // 2
    count = inputs.shape[0] * n_rep * inputs.shape[1] * n_sp * rows * 2
    part = round_up(-(-14 * ch // (2 * n_chip)), 8)
    zpart = min(part, round_up(-(-part // n_rep), 8))
    half = n_chip * part
    dma = pltpu.SemaphoreType.DMA
    vmem = pl.BlockSpec(memory_space=pltpu.VMEM)
    input_grad, weight_grad, bias_grad = pl.pallas_call(
        functools.partial(kernel, n_rep, n_sp, 1.0 / float(count) ** 0.5),
        out_shape=(
            jax.ShapeDtypeStruct(inputs.shape, BF16),
            jax.ShapeDtypeStruct(weight.shape, F32),
            jax.ShapeDtypeStruct((1, ch), F32),
        ),
        in_specs=[vmem] * 4,
        out_specs=(vmem, vmem, vmem),
        scratch_shapes=[
            pltpu.VMEM((height, packed), BF16),
            pltpu.VMEM((2, height, packed), BF16),
            pltpu.VMEM((3 * lanes, rows), BF16),
            pltpu.VMEM((3 * lanes, 6 * lanes), BF16),
            pltpu.VMEM((rows, 6 * lanes), BF16),
            pltpu.VMEM((2 * half, lanes), F32),
            pltpu.VMEM((half, lanes), F32),
            pltpu.VMEM((half, lanes), F32),
            pltpu.VMEM((max(n_chip - 1, 1), part, lanes), F32),
            pltpu.VMEM((n_rep, zpart, lanes), F32),
            pltpu.VMEM((part, lanes), F32),
            pltpu.VMEM((n_rep, zpart, lanes), F32),
            pltpu.VMEM((2, n_chip, part, lanes), F32),
            dma((2,)), dma((2,)),
            dma, dma,
            dma((n_chip,)), dma((n_chip,)),
            dma((n_rep,)), dma((n_rep,)),
            dma((n_rep,)), dma((n_rep,)),
            dma((n_chip,)), dma((n_chip,)),
            dma((n_chip,)), dma((n_chip,)),
        ],
        compiler_params=pltpu.CompilerParams(
            collective_id=0, has_side_effects=True, vmem_limit_bytes=40 * 1024 * 1024
        ),
    )(inputs, preact, grad_out, weight)
    return input_grad, weight_grad, bias_grad.reshape(ch)


def solution(mesh):
    split = P("rep", "sp", None, None)
    return jax.shard_map(
        functools.partial(on_device, mesh.shape["rep"], mesh.shape["sp"]),
        mesh=mesh,
        in_specs=(split, split, split, P()),
        out_specs=(split, P(), P()),
        check_vma=False,
    )
```
